768 devices in a mesh: pipe: 24 (over z, core), expert: 32 (over x, y).
Axes of the slice: x: 4, y: 8, z: 12, core: 2. Of those that a mesh axis runs over, the one named last changes fastest.
Arguments:
- tokens: bfloat16 [24, 4096, 3584], P('pipe', 'expert'), may hold values from -6 to 6
- routing: int32 [24, 4096, 1], P('pipe', 'expert'), may hold values from 0 to 3; in each aligned block of 128 rows (0 to 127, 128 to 255, ..., all dimensions but the last counted through in order) at most 34 rows name the same one
- scores: float32 [24, 4096, 1], P('pipe', 'expert'), may hold values from 0.2 to 1
- w_gate: bfloat16 [24, 32, 896, 512], P('pipe', 'expert'), may hold values from -0.09375 to 0.09375
- w_up: bfloat16 [24, 32, 896, 512], P('pipe', 'expert'), may hold values from -0.09375 to 0.09375
- w_down: bfloat16 [24, 32, 1024, 448], P('pipe', 'expert'), may hold values from -0.1875 to 0.1875
Outputs:
- passed: bfloat16 [24, 4096, 3584], P('pipe', 'expert')
The draws below stay inside these ranges and needn't reach their ends.
Inputs may be any that keep to these rules, and one draw needn't show every extreme that they name: `routing`: within one device's 128 tokens no expert is chosen more than 34 times, a bound that some block reaches.
All inputs are finite; a program needn't handle non-finite values.
Results may differ from the reference program's by a relative error of at most 0.0035.
Values may be sent and summed in bfloat16 or wider, within the bound.
A program may use at most 32 MiB of HBM per device.

```python
import math
import jax
import jax.numpy as jnp
import numpy as np
from jax import lax

D = 3584
FF = 1024
TOK_DEV = 128
EXPERTS = 4
CAP = 34
TOKENS = 4096
N_PIPE = 24
N_EXPERT = 32


def shard_levels(key, shape, split, smallest, largest):
    gain = 1.0
    for axis_at, shards_of in split:
        draws = jax.random.uniform(jax.random.fold_in(jax.random.fold_in(key, 6), axis_at), (shards_of,), jnp.float32, smallest / len(split), largest / len(split))
        gain = gain * jnp.repeat(jnp.exp(draws), shape[axis_at] // shards_of).reshape((-1,) + (1,) * (len(shape) - 1 - axis_at))
    return gain


def deal_out(own_key, own, number, rows, amount, top, reach, lean):
    sequence = jax.random.permutation(own_key, amount)
    heavy_load, ordinary = load_shares(amount, rows * top, reach, lean, True), load_shares(amount, rows * top, reach, lean, False)
    places = jnp.arange(amount)

    def named(lengths, rotation):
        used = int((lengths > 0).sum())
        fixed = max(1, used // 4)
        passed = fixed + (places - fixed + rotation * (used - fixed)) % max(1, amount - fixed)
        return jnp.zeros((amount,), jnp.int32).at[sequence[jnp.where(places < fixed, places, passed)]].set(jnp.asarray(lengths, jnp.int32))

    lengths = jnp.where(number % 4 == 0, named(heavy_load, number // 4), named(ordinary, number - number // 4 - 1))
    mixed = jax.random.permutation(jax.random.fold_in(own, 3), amount)
    source_of, receiver = mixed[0:amount // 2 * 2:2], mixed[1:amount // 2 * 2:2]
    slack = jnp.minimum(lengths[source_of] - 1, reach - lengths[receiver]) // 2
    slack = jnp.where((source_of == sequence[0]) | (receiver == sequence[0]) | (lengths[receiver] == 0), 0, jnp.maximum(slack, 0))
    passed = jax.random.randint(jax.random.fold_in(own, 4), (amount // 2,), 0, 1 << 20) % (slack + 1)
    lengths = lengths.at[source_of].add(-passed).at[receiver].add(passed)
    members = jnp.searchsorted(jnp.cumsum(lengths), jnp.arange(rows * top), side="right").astype(jnp.int32)
    grid = members.reshape(top, rows).T
    grid = grid[jax.random.permutation(jax.random.fold_in(own, 1), rows)]
    rotation = jax.random.randint(jax.random.fold_in(own, 2), (rows, 1), 0, top)
    return jnp.take_along_axis(grid, (jnp.arange(top)[None, :] + rotation) % top, axis=1)


def load_shares(number_of, total, bound, slope, full):
    portions = [(1 << 20) // math.isqrt(grade ** slope) + 1 for grade in range(1, number_of + 1)]
    largest = bound if full else min(bound, max(-(-total // number_of), total * portions[0] // sum(portions)))
    least = 1 if total - largest >= number_of - 1 else 0
    holding, surplus = [largest] + [least] * (number_of - 1), total - largest - least * (number_of - 1)
    while surplus > 0:
        movable = [i for i in range(1, number_of) if holding[i] < largest] or [i for i in range(1, number_of) if holding[i] < bound]
        pool, budget = sum([portions[i] for i in movable]), surplus
        for i in movable:
            addition = min(bound - holding[i], max(1, budget * portions[i] // pool), surplus)
            holding[i] = holding[i] + addition
            surplus = surplus - addition
    return np.array(holding)


def normal_values(rng, extent, spread, limit, shards=(), kind=jnp.bfloat16):
    loudness = shard_levels(rng, extent, shards, -0.22, 0.18) if shards else 1.0
    drawn = jax.random.normal(rng, extent, jnp.float32) * spread * loudness
    return jnp.minimum(jnp.maximum(drawn, -limit), limit).astype(kind)


def setup_inputs(seed: int = 0) -> dict:
    key_of = jax.random.split(jax.random.key(seed), 7)
    tokens = normal_values(key_of[0], (N_PIPE, TOKENS, D), 1.0, 6.0, ((0, 24), (1, 32)))
    routing_keys = jax.random.split(jax.random.fold_in(key_of[1], 1), N_PIPE * TOKENS // TOK_DEV)
    routing_turns = jax.random.permutation(jax.random.fold_in(key_of[1], 3), N_PIPE * TOKENS // TOK_DEV)
    routing = jax.vmap(lambda own, number: deal_out(jax.random.fold_in(key_of[1], 2), own, number, TOK_DEV, EXPERTS, 1, CAP, 2))(routing_keys, routing_turns).reshape((N_PIPE, TOKENS, 1))
    scores = jnp.clip(0.2 + 0.8 * jax.random.uniform(key_of[2], (N_PIPE, TOKENS, 1), jnp.float32) ** shard_levels(key_of[2], (N_PIPE, TOKENS, 1), ((0, 24), (1, 32)), -0.2, 0.2), 0.2, 1.0)
    w_gate = normal_values(key_of[3], (N_PIPE, N_EXPERT, D // 4, FF // 2), D ** -0.5, 0.09375, ((0, 24), (1, 32)))
    w_up = normal_values(key_of[4], (N_PIPE, N_EXPERT, D // 4, FF // 2), D ** -0.5, 0.09375, ((0, 24), (1, 32)))
    w_down = normal_values(key_of[5], (N_PIPE, N_EXPERT, FF, D // 8), FF ** -0.5, 0.1875, ((0, 24), (1, 32)))
    return dict(tokens=tokens, routing=routing, scores=scores, w_gate=w_gate, w_up=w_up, w_down=w_down)


def assemble(gate_blocks, up_blocks, down_blocks):
    experts_here = gate_blocks.shape[0] // 8
    quarter_rows = gate_blocks.shape[1]
    half_cols = gate_blocks.shape[2]

    def joined(blocks):
        shaped = blocks.reshape(experts_here, 4, 2, quarter_rows, half_cols)
        return shaped.transpose(0, 1, 3, 2, 4).reshape(experts_here, 4 * quarter_rows, 2 * half_cols)

    eighth = down_blocks.shape[2]
    hidden_units = down_blocks.shape[1]
    down_full = down_blocks.reshape(experts_here, 8, hidden_units, eighth).transpose(0, 2, 1, 3)
    return joined(gate_blocks), joined(up_blocks), down_full.reshape(experts_here, hidden_units, 8 * eighth)


def reference(tokens, routing, scores, w_gate, w_up, w_down):
    groups = N_EXPERT
    capacity = CAP
    choice_ids = routing[..., 0].reshape(N_PIPE, groups, TOK_DEV)
    onehot = (choice_ids[..., None] == jnp.arange(EXPERTS, dtype=jnp.int32)).astype(jnp.int32)
    slot_index = jnp.sum(jnp.cumsum(onehot, axis=2) * onehot, axis=3) - 1
    device = jnp.arange(groups, dtype=jnp.int32)[None, :, None]
    dest_row = (choice_ids * (groups * capacity) + device * capacity + slot_index).astype(jnp.int32)
    dest_row = dest_row.reshape(N_PIPE, TOKENS)

    def section(section_args):
        x_rows, dest_rows, router_w, gate_blocks, up_blocks, down_blocks = section_args
        gate_full, up_full, down_full = assemble(gate_blocks, up_blocks, down_blocks)
        buffer = jnp.zeros((EXPERTS * groups * capacity, D), jnp.bfloat16).at[dest_rows].set(x_rows)
        buffer = buffer.reshape(EXPERTS, groups * capacity, D)

        def expert(operands):
            row_block, gate_mat, up_mat, down_mat = operands
            gate = jnp.dot(row_block, gate_mat, preferred_element_type=jnp.float32)
            up_val = jnp.dot(row_block, up_mat, preferred_element_type=jnp.float32)
            hidden = (jax.nn.silu(gate) * up_val).astype(jnp.bfloat16)
            return jnp.dot(hidden, down_mat, preferred_element_type=jnp.float32).astype(jnp.bfloat16)

        expert_out = lax.map(expert, (buffer, gate_full, up_full, down_full)).reshape(-1, D)
        gathered = expert_out[dest_rows]
        return (x_rows.astype(jnp.float32) + router_w[:, None] * gathered.astype(jnp.float32)).astype(jnp.bfloat16)

    layer_out = lax.map(section, (tokens, dest_row, scores[..., 0], w_gate, w_up, w_down))
    zero_rows = jnp.zeros((1, TOKENS, D), jnp.bfloat16)
    below = jnp.concatenate([zero_rows, layer_out[:-1]], axis=0)
    above = jnp.concatenate([layer_out[1:], zero_rows], axis=0)
    parity = (jnp.arange(N_PIPE, dtype=jnp.int32) % 2)[:, None, None]
    return jnp.where(parity == 0, above, below)
```

```python
import functools
import jax
import jax.numpy as jnp
from jax import lax
from jax.experimental import pallas as pl
from jax.experimental.pallas import tpu as pltpu
from jax.sharding import PartitionSpec as P

MESH = pl.DeviceIdType.MESH
BF = jnp.bfloat16
F32 = jnp.float32

D = 3584
TOK = 128
QD = 896
HB = 512
STAGES = 4
ROWS = TOK // STAGES
FOLD = ROWS * 7 // 2
NEEDS = ((0, 1), (0, 1, 2), (1, 2, 3), (2, 3))


def dot(a, b):
    return jnp.dot(a, b, preferred_element_type=F32)


def iota(shape, axis):
    return lax.broadcasted_iota(jnp.int32, shape, axis)


def onehot(cond):
    return jnp.where(cond, 1.0, 0.0).astype(F32)


def kernel(tok, routing, scores, w_gate, w_up, w_down, out,
           rq, xa, bnd, part, psend, relay, near, hid, lhs, lhd, wgu, wd, wdn,
           osend, oback, toks, dests, scos, dmine, smine, oall,
           s_loc, s_w, r_w, s_b, r_b, s_sib, r_sib, s_tok, r_tok, s_p, r_p,
           s_h, r_h, s_o, r_o):
    pipe = lax.axis_index("pipe")
    place = lax.axis_index("expert")
    x, y = place // 8, place % 8
    a, b = y // 2, y % 2
    sig = 1 - 2 * b
    other = pipe + 1 - 2 * (pipe % 2)

    def m8(v):
        return lax.rem(v + 16, 8)

    def on_line(v):
        return (pipe, x * 8 + m8(v))

    def on_cross(v):
        return (pipe, lax.rem(x + v + 4, 4) * 8 + y)

    barrier = pltpu.get_barrier_semaphore()
    for d in range(1, 8):
        pl.semaphore_signal(barrier, inc=1, device_id=on_line(y + d), device_id_type=MESH)
    for d in range(1, 4):
        pl.semaphore_signal(barrier, inc=1, device_id=on_cross(d), device_id_type=MESH)
    for d in range(8):
        pl.semaphore_signal(barrier, inc=1, device_id=(other, x * 8 + d), device_id_type=MESH)

    pending = []

    def remote(src, dst, ssem, rsem, device):
        return pltpu.make_async_remote_copy(
            src_ref=src, dst_ref=dst, send_sem=ssem, recv_sem=rsem,
            device_id=device, device_id_type=MESH)

    def send(*args):
        copy = remote(*args)
        copy.start()
        pending.append(copy)
        return copy

    def sent(copies):
        for copy in copies:
            copy.wait_send()
            pending[:] = [c for c in pending if c is not copy]

    local = []
    for n, (src, dst) in enumerate(
            ((w_gate, wgu.at[0, 0]), (w_up, wgu.at[0, 1]), (w_down, wdn))):
        copy = pltpu.make_async_copy(src, dst, s_loc.at[n])
        copy.start()
        local.append(copy)

    rel = lax.rem(routing[...] - x + 4, 4)
    key = jnp.where(rel == 2, 3, jnp.where(rel == 3, 2, rel))
    lane = iota((TOK, TOK), 1)
    sub = iota((TOK, TOK), 0)
    member = onehot(key == lane)
    member16 = member.astype(BF)
    before = dot(onehot(lane < sub).astype(BF), member16)
    total = dot(jnp.ones((TOK, TOK), BF), member16)
    start = dot(total.astype(BF), onehot(sub < lane).astype(BF))
    dest = jnp.sum((start + before) * member, axis=1, keepdims=True)
    dest = jnp.broadcast_to(dest, (TOK, TOK))
    dmine[...] = dest
    smine[...] = jnp.broadcast_to(scores[...], (TOK, TOK))
    first = jnp.sum(
        jnp.where(lane[:8] == sub[:8], start[:8], 0.0), axis=1, keepdims=True)
    bnd[y] = jnp.broadcast_to(first, (8, TOK))
    place_of = onehot(dest == lane.astype(F32)).T.astype(BF)

    pl.semaphore_wait(barrier, 18)

    def send_w(n, slot):
        src = (w_gate, w_up, wd.at[0])[n]
        dst = (wgu.at[slot, 0], wgu.at[slot, 1], wd.at[slot])[n]
        to = (-1, 1, 2)[slot - 1]
        return send(src, dst, s_w.at[n, slot - 1], r_w.at[n, slot - 1], on_cross(to))

    def wait_w(n, slot):
        dst = (wgu.at[slot, 0], wgu.at[slot, 1], wd.at[slot])[n]
        src = (w_gate, w_up, wd.at[0])[n]
        remote(src, dst, s_w.at[n, slot - 1], r_w.at[n, slot - 1], on_cross(1)).wait_recv()

    first_w = [send_w(n, slot) for n in (0, 1) for slot in (1, 2)]

    kinds = (sig, 2 * sig, -sig, -3 * sig)
    sources = [m8(y + v) for v in
               (sig, -2 * sig, -sig, -3 * sig, 3 * sig, 2 * sig, 4 * sig)]

    for d in range(1, 8):
        send(bnd.at[y], bnd.at[y], s_b.at[d - 1], r_b.at[d - 1], on_line(y + d))

    for i in range(STAGES):
        rows = pl.ds(i * ROWS, ROWS)
        for q in range(4):
            rq[q, rows, :] = dot(
                place_of[i * ROWS:(i + 1) * ROWS], tok[:, q * QD:(q + 1) * QD]).astype(BF)
        for k in (3, 1, 2, 0):
            to = m8(y + kinds[k])
            send(rq.at[to // 2, rows], xa.at[y, rows],
                 s_tok.at[i, k], r_tok.at[i, k], on_line(to))
        xa[y, rows, :] = rq[a, rows, :]

    send(tok, toks, s_sib.at[0], r_sib.at[0], (other, place))
    send(dmine, dests, s_sib.at[1], r_sib.at[1], (other, place))
    send(smine, scos, s_sib.at[2], r_sib.at[2], (other, place))

    def tok_arrived(i, k):
        at = xa.at[sources[k], pl.ds(i * ROWS, ROWS)]
        remote(at, at, s_tok.at[i, k], r_tok.at[i, k], on_line(y + 1)).wait_recv()
        return at

    def forward(i):
        for k in (2, 1, 3):
            at = tok_arrived(i, k)
            send(at, at, s_tok.at[i, k + 3], r_tok.at[i, k + 3], on_line(y + sig))

    def order_down():
        for copy in local:
            copy.wait()
        c = iota((448, 512), 0)
        l = iota((448, 512), 1)
        from_col = jnp.where(l < 384, l + 64 * b, l % 64 + 384 * (1 - b))
        pick = onehot(c == from_col).astype(BF)

        @pl.loop(0, 4)
        def _(r):
            at = pl.ds(pl.multiple_of(r * 256, 256), 256)
            wd[0, at, :] = dot(wdn[at, :], pick).astype(BF)

    def mask(s, i, j):
        row = iota((ROWS, TOK), 0).astype(F32) + float(i * ROWS)
        low = bnd[s, j:j + 1, :]
        high = bnd[s, j + 1:j + 2, :]
        return onehot((row >= low) & (row < high)).astype(BF)

    def partial(i):
        rows = pl.ds(i * ROWS, ROWS)
        for n, j in enumerate(NEEDS[i]):
            @pl.loop(0, 8)
            def _(s):
                m = mask(s, i, j)
                at = pl.ds(pl.multiple_of(s * ROWS, ROWS), ROWS)
                for c in range(7):
                    lanes = pl.ds(c * TOK, TOK)
                    lhs[n, at, lanes] = xa[s, rows, lanes] * m

        @pl.loop(0, 4)
        def _(c):
            at = pl.ds(pl.multiple_of((c % 2) * 256, 256), 256)
            acc = None
            for n, j in enumerate(NEEDS[i]):
                term = dot(lhs[n], wgu[j, c // 2, :, at])
                acc = term if acc is None else acc + term
            acc = acc.reshape(8, ROWS, 256)
            col = pl.ds(pl.multiple_of(c * 256, 256), 256)
            part[:, rows, col] = acc
            psend[:, rows, col] = acc.astype(BF)

    far = 2 * lax.rem(a + 2, 4)
    up = 2 * lax.rem(a + 1, 4)
    down = 2 * lax.rem(a + 3, 4)

    def p_copy(i, k):
        rows = pl.ds(i * ROWS, ROWS)
        src = (far, far + 1, up + 1, down, up, down + 1)[k]
        dst = (relay.at[0, rows], relay.at[1, rows], near.at[0, 1, rows],
               near.at[1, 0, rows], near.at[0, 0, rows], near.at[1, 1, rows])[k]
        to = (2, -2, 2, -2, 2, -2)[k]
        return remote(psend.at[src, rows], dst, s_p.at[i, k], r_p.at[i, k], on_line(y + to))

    def p_start(i, ks):
        for k in ks:
            copy = p_copy(i, k)
            copy.start()
            pending.append(copy)

    def relayed(i):
        rows = pl.ds(i * ROWS, ROWS)
        for k, s in ((0, up), (1, down + 1)):
            p_copy(i, k).wait_recv()
            psend[s, rows, :] = (
                part[s, rows, :] + relay[k, rows, :].astype(F32)).astype(BF)
            p_start(i, (k + 4,))

    def h_copy(i, t, way):
        step = (1, -1)[way]
        owner = m8(y - step * (t - 1))
        rows = pl.ds(i * ROWS, ROWS)
        src = 2 * (owner // 2)
        if t == 4:
            at = hid.at[owner % 2, pl.ds(src + way, 1), rows]
        else:
            at = hid.at[owner % 2, pl.ds(src, 2), rows]
        return remote(at, at, s_h.at[i, t - 1, way], r_h.at[i, t - 1, way], on_line(y + step))

    def h_start(i, t):
        for way in (0, 1):
            copy = h_copy(i, t, way)
            copy.start()
            pending.append(copy)

    def h_arrived(i, t):
        for way in (0, 1):
            step = (1, -1)[way]
            owner = m8(y - step * t)
            rows = pl.ds(i * ROWS, ROWS)
            src = 2 * (owner // 2)
            if t == 4:
                at = hid.at[owner % 2, pl.ds(src + way, 1), rows]
            else:
                at = hid.at[owner % 2, pl.ds(src, 2), rows]
            remote(at, at, s_h.at[i, t - 1, way], r_h.at[i, t - 1, way],
                   on_line(y + step)).wait_recv()

    def hidden(i):
        rows = pl.ds(i * ROWS, ROWS)
        for k in (2, 3, 4, 5):
            p_copy(i, k).wait_recv()
        for k in (0, 1):
            s = 2 * a + k
            whole = (part[s, rows, :] + near[0, k, rows, :].astype(F32)
                     + near[1, k, rows, :].astype(F32))
            g, u = whole[:, :HB], whole[:, HB:]
            hid[b, s, rows, :] = (g / (1.0 + jnp.exp(-g)) * u).astype(BF)
        h_start(i, 1)

    def pass_on(i, t):
        h_arrived(i, t - 1)
        h_start(i, t)

    def expert_out(i):
        h_arrived(i, 4)
        rows = pl.ds(i * ROWS, ROWS)
        for n, j in enumerate(NEEDS[i]):
            @pl.loop(0, 8)
            def _(s):
                m = mask(s, i, j)
                at = pl.ds(pl.multiple_of(s * ROWS, ROWS), ROWS)
                for c in range(8):
                    lhd[n, at, pl.ds(c * TOK, TOK)] = (
                        hid[c // 4, s, rows, pl.ds((c % 4) * TOK, TOK)] * m)

        keep = iota((16, TOK), 1) // 64 == b
        half = ROWS // 2
        base = i * FOLD

        @pl.loop(0, 2)
        def _(c):
            at = pl.ds(pl.multiple_of(c * 256, 256), 256)
            acc = None
            for n, j in enumerate(NEEDS[i]):
                term = dot(lhd[n], wd[j, :, at])
                acc = term if acc is None else acc + term
            acc = acc.reshape(8, ROWS, 256)
            low = base + c * (2 * ROWS)
            osend[:, pl.ds(pl.multiple_of(low, 16), ROWS), :] = acc[:, :, :TOK].astype(BF)

            @pl.when(c == 0)
            def _():
                osend[:, pl.ds(base + ROWS, ROWS), :] = acc[:, :, TOK:].astype(BF)

            @pl.when(c == 1)
            def _():
                folded = jnp.where(keep[None], acc[:, :half, TOK:], acc[:, half:, TOK:])
                osend[:, pl.ds(base + 3 * ROWS, half), :] = folded.astype(BF)

        fold = pl.ds(base, FOLD)
        for d in (4, 3, 5, 2, 6, 1, 7, 0):
            to = m8(y + d)
            send(osend.at[to, fold], oback.at[y, fold],
                 s_o.at[i, d], r_o.at[i, d], (other, x * 8 + to))

    def collect(i):
        base = i * FOLD
        fold = pl.ds(base, FOLD)
        for d in range(8):
            at = oback.at[m8(y - d), fold]
            remote(at, at, s_o.at[i, d], r_o.at[i, d], (other, place)).wait_recv()
        half = ROWS // 2
        low_lanes = iota((half, TOK), 1) < 64
        for m in range(4):
            col = m * QD
            for c in range(3):
                r = pl.ds(base + c * ROWS, ROWS)
                oall[pl.ds(i * ROWS, ROWS), pl.ds(col + c * TOK, TOK)] = oback[2 * m, r, :]
                oall[pl.ds(i * ROWS, ROWS), pl.ds(col + 512 + c * TOK, TOK)] = (
                    oback[2 * m + 1, r, :])
            r = pl.ds(base + 3 * ROWS, half)
            even = oback[2 * m, r, :].astype(F32)
            odd = oback[2 * m + 1, r, :].astype(F32)
            oall[pl.ds(i * ROWS, half), pl.ds(col + 384, TOK)] = (
                jnp.where(low_lanes, even, odd).astype(BF))
            oall[pl.ds(i * ROWS + half, half), pl.ds(col + 384, TOK)] = (
                pltpu.roll(jnp.where(low_lanes, odd, even), 64, 1).astype(BF))

    for i in range(STAGES):
        forward(i)
        if i == 0:
            order_down()
            for d in range(1, 8):
                at = bnd.at[m8(y - d)]
                remote(at, at, s_b.at[d - 1], r_b.at[d - 1], on_line(y + d)).wait_recv()
    for i in range(STAGES):
        for k in (0, 4, 5, 6):
            tok_arrived(i, k)

    sent(first_w)
    last_w = [send_w(n, 3) for n in (0, 1)]
    for n in (0, 1):
        for slot in (1, 2):
            wait_w(n, slot)
    partial(0)
    p_start(0, range(4))
    partial(1)
    p_start(1, range(4))
    relayed(0)
    relayed(1)
    hidden(0)
    pass_on(0, 2)
    pass_on(0, 3)
    hidden(1)
    pass_on(0, 4)
    pass_on(1, 2)
    sent(last_w)
    down_w = [send_w(2, slot) for slot in (1, 2)]
    for n in (0, 1):
        wait_w(n, 3)
    partial(2)
    p_start(2, range(4))
    partial(3)
    p_start(3, range(4))
    pass_on(1, 3)
    pass_on(1, 4)
    relayed(2)
    relayed(3)
    sent(down_w)
    send_w(2, 3)
    hidden(2)
    pass_on(2, 2)
    pass_on(2, 3)
    hidden(3)
    pass_on(2, 4)
    pass_on(3, 2)
    for slot in (1, 2):
        wait_w(2, slot)
    expert_out(0)
    expert_out(1)
    pass_on(3, 3)
    pass_on(3, 4)
    wait_w(2, 3)
    expert_out(2)
    expert_out(3)
    remote(tok, toks, s_sib.at[0], r_sib.at[0], (other, place)).wait_recv()
    remote(dmine, dests, s_sib.at[1], r_sib.at[1], (other, place)).wait_recv()
    remote(smine, scos, s_sib.at[2], r_sib.at[2], (other, place)).wait_recv()
    for i in range(STAGES):
        collect(i)

    back = onehot(dests[...] == lane.astype(F32)).astype(BF)

    @pl.loop(0, 7)
    def _(c):
        at = pl.ds(pl.multiple_of(c * 512, 512), 512)
        gain = scos[...]
        moved = dot(back, oall[:, at])
        gain = jnp.concatenate([gain] * 4, axis=1)
        out[:, at] = (toks[:, at].astype(F32) + gain * moved).astype(BF)

    for copy in pending:
        copy.wait_send()


def body(tokens, routing, scores, w_gate, w_up, w_down):
    vmem = pl.BlockSpec(memory_space=pltpu.VMEM)
    hbm = pl.BlockSpec(memory_space=pl.ANY)
    dma = pltpu.SemaphoreType.DMA
    result = pl.pallas_call(
        kernel,
        out_shape=jax.ShapeDtypeStruct((TOK, D), BF),
        in_specs=[vmem, vmem, vmem, hbm, hbm, hbm],
        out_specs=vmem,
        scratch_shapes=[
            pltpu.VMEM((4, TOK, QD), BF),
            pltpu.VMEM((8, TOK, QD), BF),
            pltpu.VMEM((8, 8, TOK), F32),
            pltpu.VMEM((8, TOK, 2 * HB), F32),
            pltpu.VMEM((8, TOK, 2 * HB), BF),
            pltpu.VMEM((2, TOK, 2 * HB), BF),
            pltpu.VMEM((2, 2, TOK, 2 * HB), BF),
            pltpu.VMEM((2, 8, TOK, HB), BF),
            pltpu.VMEM((3, 8 * ROWS, QD), BF),
            pltpu.VMEM((3, 8 * ROWS, 2 * HB), BF),
            pltpu.VMEM((4, 2, QD, HB), BF),
            pltpu.VMEM((4, 2 * HB, 512), BF),
            pltpu.VMEM((2 * HB, 448), BF),
            pltpu.VMEM((8, STAGES * FOLD, TOK), BF),
            pltpu.VMEM((8, STAGES * FOLD, TOK), BF),
            pltpu.VMEM((TOK, D), BF),
            pltpu.VMEM((TOK, TOK), F32),
            pltpu.VMEM((TOK, TOK), F32),
            pltpu.VMEM((TOK, TOK), F32),
            pltpu.VMEM((TOK, TOK), F32),
            pltpu.VMEM((TOK, D), BF),
            dma((3,)),
            dma((3, 3)), dma((3, 3)),
            dma((7,)), dma((7,)),
            dma((3,)), dma((3,)),
            dma((STAGES, 7)), dma((STAGES, 7)),
            dma((STAGES, 6)), dma((STAGES, 6)),
            dma((STAGES, 4, 2)), dma((STAGES, 4, 2)),
            dma((STAGES, 8)), dma((STAGES, 8)),
        ],
        compiler_params=pltpu.CompilerParams(
            collective_id=0, has_side_effects=True, vmem_limit_bytes=52 * 2**20),
        cost_estimate=pl.CostEstimate(
            flops=8 * 10**9, bytes_accessed=6 * 10**6, transcendentals=131072),
    )(tokens[0], routing[0], scores[0], w_gate[0, 0], w_up[0, 0], w_down[0, 0])
    return result[None]


def solution(mesh):
    return jax.shard_map(
        body,
        mesh=mesh,
        in_specs=(
            P("pipe", "expert", None),
            P("pipe", "expert", None),
            P("pipe", "expert", None),
            P("pipe", "expert", None, None),
            P("pipe", "expert", None, None),
            P("pipe", "expert", None, None),
        ),
        out_specs=P("pipe", "expert", None),
        check_vma=False,
    )
```

```python
import functools
import jax
import jax.numpy as jnp
from jax import lax
from jax.experimental import pallas as pl
from jax.experimental.pallas import tpu as pltpu
from jax.sharding import PartitionSpec as P

MESH = pl.DeviceIdType.MESH
BF = jnp.bfloat16
F32 = jnp.float32

D = 3584
TOK = 128
QD = 896
HB = 512
STAGES = 4
ROWS = TOK // STAGES
FOLD = ROWS * 7 // 2
NEEDS = ((0, 1), (0, 1, 2), (1, 2, 3), (2, 3))
ORDER = (
    ("F", 0), ("D",), ("B",), ("F", 1), ("F", 2), ("W", 0), ("F", 3),
    ("T", 0), ("T", 1), ("T", 2), ("T", 3), ("W", 1), ("V", 2, (0, 1)),
    ("P", 0), ("P", 1), ("R", 0), ("R", 1), ("H", 0), ("G", 0, 2),
    ("H", 1), ("G", 0, 3), ("G", 1, 2),
    ("X", 0, (2, 3)), ("X", 1, (2, 3)),
    ("P", 2), ("P", 3), ("G", 0, 4), ("G", 1, 3), ("R", 2), ("G", 1, 4), ("R", 3),
    ("H", 2), ("G", 2, 2), ("H", 3), ("G", 2, 3), ("G", 3, 2), ("W", 2),
    ("O", 0), ("G", 2, 4), ("G", 3, 3), ("O", 1), ("G", 3, 4),
    ("X", 2, (2, 3)), ("O", 2), ("O", 3),
    ("S",), ("C", 0), ("C", 1), ("C", 2), ("C", 3),
)


def dot(a, b):
    return jnp.dot(a, b, preferred_element_type=F32)


def iota(shape, axis):
    return lax.broadcasted_iota(jnp.int32, shape, axis)


def onehot(cond):
    return jnp.where(cond, 1.0, 0.0).astype(F32)


def kernel(tok, routing, scores, w_gate, w_up, w_down, out,
           rq, xa, bnd, part, psend, relay, near, hid, lhs, lhd, wgu, wd,
           osend, oback, toks, dests, scos, dmine, smine, oall,
           s_loc, s_w, r_w, s_b, r_b, s_sib, r_sib, s_tok, r_tok, s_p, r_p,
           s_h, r_h, s_o, r_o):
    pipe = lax.axis_index("pipe")
    place = lax.axis_index("expert")
    x, y = place // 8, place % 8
    a, b = y // 2, y % 2
    sig = 1 - 2 * b
    other = pipe + 1 - 2 * (pipe % 2)

    def m8(v):
        return lax.rem(v + 16, 8)

    def on_line(v):
        return (pipe, x * 8 + m8(v))

    def on_cross(v):
        return (pipe, lax.rem(x + v + 4, 4) * 8 + y)

    barrier = pltpu.get_barrier_semaphore()
    for d in range(1, 8):
        pl.semaphore_signal(barrier, inc=1, device_id=on_line(y + d), device_id_type=MESH)
    for d in range(1, 4):
        pl.semaphore_signal(barrier, inc=1, device_id=on_cross(d), device_id_type=MESH)
    for d in range(8):
        pl.semaphore_signal(barrier, inc=1, device_id=(other, x * 8 + d), device_id_type=MESH)

    pending = []

    def remote(src, dst, ssem, rsem, device):
        return pltpu.make_async_remote_copy(
            src_ref=src, dst_ref=dst, send_sem=ssem, recv_sem=rsem,
            device_id=device, device_id_type=MESH)

    def send(*args):
        copy = remote(*args)
        copy.start()
        pending.append(copy)
        return copy

    local = []
    for n, (src, dst) in enumerate(
            ((w_gate, wgu.at[0, 0]), (w_up, wgu.at[0, 1]), (w_down, wd.at[0]))):
        copy = pltpu.make_async_copy(src, dst, s_loc.at[n])
        copy.start()
        local.append(copy)

    rel = lax.rem(routing[...] - x + 4, 4)
    key = jnp.where(rel == 2, 3, jnp.where(rel == 3, 2, rel))
    lane = iota((TOK, TOK), 1)
    sub = iota((TOK, TOK), 0)
    member = onehot(key == lane)
    member16 = member.astype(BF)
    before = dot(onehot(lane < sub).astype(BF), member16)
    total = dot(jnp.ones((TOK, TOK), BF), member16)
    start = dot(total.astype(BF), onehot(sub < lane).astype(BF))
    dest = jnp.sum((start + before) * member, axis=1, keepdims=True)
    dest = jnp.broadcast_to(dest, (TOK, TOK))
    dmine[...] = dest
    smine[...] = jnp.broadcast_to(scores[...], (TOK, TOK))
    first = jnp.sum(
        jnp.where(lane[:8] == sub[:8], start[:8], 0.0), axis=1, keepdims=True)
    bnd[y] = jnp.broadcast_to(first, (8, TOK))
    place_of = onehot(dest == lane.astype(F32)).T.astype(BF)

    pl.semaphore_wait(barrier, 18)

    def w_copy(n, k):
        own = (w_gate, w_up, w_down)[n]
        held = [None] + [(wgu.at[j, 0], wgu.at[j, 1], wd.at[j])[n] for j in (1, 2, 3)]
        size = (QD // 2, QD // 2, 224)[n]
        halves = (pl.ds(0, size), pl.ds(size, size))
        src = (own, own, held[1].at[halves[0]], held[2].at[halves[1]])[k]
        dst = (held[1], held[2], held[3].at[halves[0]], held[3].at[halves[1]])[k]
        return remote(src, dst, s_w.at[n, k], r_w.at[n, k], on_cross((-1, 1, -1, 1)[k]))

    def w_start(n, ks):
        for k in ks:
            copy = w_copy(n, k)
            copy.start()
            pending.append(copy)

    def w_wait(n, ks):
        for k in ks:
            w_copy(n, k).wait_recv()

    for n in (0, 1):
        w_start(n, (0, 1))

    kinds = (sig, 2 * sig, -sig, -3 * sig)
    sources = [m8(y + v) for v in
               (sig, -2 * sig, -sig, -3 * sig, 3 * sig, 2 * sig, 4 * sig)]

    for d in range(1, 8):
        send(bnd.at[y], bnd.at[y], s_b.at[d - 1], r_b.at[d - 1], on_line(y + d))

    for i in range(STAGES):
        rows = pl.ds(i * ROWS, ROWS)
        for q in range(4):
            rq[q, rows, :] = dot(
                place_of[i * ROWS:(i + 1) * ROWS], tok[:, q * QD:(q + 1) * QD]).astype(BF)
        for k in (3, 1, 2, 0):
            to = m8(y + kinds[k])
            send(rq.at[to // 2, rows], xa.at[y, rows],
                 s_tok.at[i, k], r_tok.at[i, k], on_line(to))
        xa[y, rows, :] = rq[a, rows, :]

    send(tok, toks, s_sib.at[0], r_sib.at[0], (other, place))
    send(dmine, dests, s_sib.at[1], r_sib.at[1], (other, place))
    send(smine, scos, s_sib.at[2], r_sib.at[2], (other, place))

    def tok_arrived(i, k):
        at = xa.at[sources[k], pl.ds(i * ROWS, ROWS)]
        remote(at, at, s_tok.at[i, k], r_tok.at[i, k], on_line(y + 1)).wait_recv()
        return at

    def forward(i):
        for k in (2, 1, 3):
            at = tok_arrived(i, k)
            send(at, at, s_tok.at[i, k + 3], r_tok.at[i, k + 3], on_line(y + sig))

    def own_weights():
        for copy in local:
            copy.wait()

    def mask(s, i, j):
        row = iota((ROWS, TOK), 0).astype(F32) + float(i * ROWS)
        low = bnd[s, j:j + 1, :]
        high = bnd[s, j + 1:j + 2, :]
        return onehot((row >= low) & (row < high)).astype(BF)

    def partial(i):
        rows = pl.ds(i * ROWS, ROWS)
        for n, j in enumerate(NEEDS[i]):
            @pl.loop(0, 8)
            def _(s):
                m = mask(s, i, j)
                at = pl.ds(pl.multiple_of(s * ROWS, ROWS), ROWS)
                for c in range(7):
                    lanes = pl.ds(c * TOK, TOK)
                    lhs[n, at, lanes] = xa[s, rows, lanes] * m

        @pl.loop(0, 4)
        def _(c):
            at = pl.ds(pl.multiple_of((c % 2) * 256, 256), 256)
            acc = None
            for n, j in enumerate(NEEDS[i]):
                term = dot(lhs[n], wgu[j, c // 2, :, at])
                acc = term if acc is None else acc + term
            acc = acc.reshape(8, ROWS, 256)
            col = pl.ds(pl.multiple_of(c * 256, 256), 256)
            part[:, rows, col] = acc
            psend[:, rows, col] = acc.astype(BF)

    far = 2 * lax.rem(a + 2, 4)
    up = 2 * lax.rem(a + 1, 4)
    down = 2 * lax.rem(a + 3, 4)

    def p_copy(i, k):
        rows = pl.ds(i * ROWS, ROWS)
        src = (far, far + 1, up + 1, down, up, down + 1)[k]
        dst = (relay.at[0, rows], relay.at[1, rows], near.at[0, 1, rows],
               near.at[1, 0, rows], near.at[0, 0, rows], near.at[1, 1, rows])[k]
        to = (2, -2, 2, -2, 2, -2)[k]
        return remote(psend.at[src, rows], dst, s_p.at[i, k], r_p.at[i, k], on_line(y + to))

    def p_start(i, ks):
        for k in ks:
            copy = p_copy(i, k)
            copy.start()
            pending.append(copy)

    def relayed(i):
        rows = pl.ds(i * ROWS, ROWS)
        for k, s in ((0, up), (1, down + 1)):
            p_copy(i, k).wait_recv()
            psend[s, rows, :] = (
                part[s, rows, :] + relay[k, rows, :].astype(F32)).astype(BF)
            p_start(i, (k + 4,))

    def h_copy(i, t, way):
        step = (1, -1)[way]
        owner = m8(y - step * (t - 1))
        rows = pl.ds(i * ROWS, ROWS)
        src = 2 * (owner // 2)
        if t == 4:
            at = hid.at[owner % 2, pl.ds(src + way, 1), rows]
        else:
            at = hid.at[owner % 2, pl.ds(src, 2), rows]
        return remote(at, at, s_h.at[i, t - 1, way], r_h.at[i, t - 1, way], on_line(y + step))

    def h_start(i, t):
        for way in (0, 1):
            copy = h_copy(i, t, way)
            copy.start()
            pending.append(copy)

    def h_arrived(i, t):
        for way in (0, 1):
            step = (1, -1)[way]
            owner = m8(y - step * t)
            rows = pl.ds(i * ROWS, ROWS)
            src = 2 * (owner // 2)
            if t == 4:
                at = hid.at[owner % 2, pl.ds(src + way, 1), rows]
            else:
                at = hid.at[owner % 2, pl.ds(src, 2), rows]
            remote(at, at, s_h.at[i, t - 1, way], r_h.at[i, t - 1, way],
                   on_line(y + step)).wait_recv()

    def hidden(i):
        rows = pl.ds(i * ROWS, ROWS)
        for k in (2, 3, 4, 5):
            p_copy(i, k).wait_recv()
        for k in (0, 1):
            s = 2 * a + k
            whole = (part[s, rows, :] + near[0, k, rows, :].astype(F32)
                     + near[1, k, rows, :].astype(F32))
            g, u = whole[:, :HB], whole[:, HB:]
            hid[b, s, rows, :] = (g / (1.0 + jnp.exp(-g)) * u).astype(BF)
        h_start(i, 1)

    def pass_on(i, t):
        h_arrived(i, t - 1)
        h_start(i, t)

    def expert_out(i):
        h_arrived(i, 4)
        rows = pl.ds(i * ROWS, ROWS)
        for n, j in enumerate(NEEDS[i]):
            @pl.loop(0, 8)
            def _(s):
                m = mask(s, i, j)
                at = pl.ds(pl.multiple_of(s * ROWS, ROWS), ROWS)
                for c in range(8):
                    lhd[n, at, pl.ds(c * TOK, TOK)] = (
                        hid[c // 4, s, rows, pl.ds((c % 4) * TOK, TOK)] * m)

        keep = iota((16, TOK), 1) // 64 == b
        half = ROWS // 2
        base = i * FOLD

        def term(n, cols):
            return lax.dot_general(
                lhd[n], cols, (((1,), (1,)), ((), ())), preferred_element_type=F32)

        @pl.loop(0, 3)
        def _(c):
            at = pl.ds(pl.multiple_of(c * TOK + 64 * b, 64), TOK)
            acc = sum(term(n, wd[j, at, :]) for n, j in enumerate(NEEDS[i]))
            low = pl.multiple_of(base + c * ROWS, 16)
            osend[:, pl.ds(low, ROWS), :] = acc.reshape(8, ROWS, TOK).astype(BF)

        at = pl.ds(pl.multiple_of(384 * (1 - b), 64), 64)
        acc = 0.0
        for n, j in enumerate(NEEDS[i]):
            rest = wd[j, at, :]
            acc = acc + term(n, jnp.concatenate([rest, rest], axis=0))
        acc = acc.reshape(8, ROWS, TOK)
        folded = jnp.where(keep[None], acc[:, :half], acc[:, half:])
        osend[:, pl.ds(base + 3 * ROWS, half), :] = folded.astype(BF)

        fold = pl.ds(base, FOLD)
        for d in (4, 3, 5, 2, 6, 1, 7, 0):
            to = m8(y + d)
            send(osend.at[to, fold], oback.at[y, fold],
                 s_o.at[i, d], r_o.at[i, d], (other, x * 8 + to))

    def collect(i):
        base = i * FOLD
        fold = pl.ds(base, FOLD)
        for d in range(8):
            at = oback.at[m8(y - d), fold]
            remote(at, at, s_o.at[i, d], r_o.at[i, d], (other, place)).wait_recv()
        half = ROWS // 2
        low_lanes = iota((half, TOK), 1) < 64
        for m in range(4):
            col = m * QD
            for c in range(3):
                r = pl.ds(base + c * ROWS, ROWS)
                oall[pl.ds(i * ROWS, ROWS), pl.ds(col + c * TOK, TOK)] = oback[2 * m, r, :]
                oall[pl.ds(i * ROWS, ROWS), pl.ds(col + 512 + c * TOK, TOK)] = (
                    oback[2 * m + 1, r, :])
            r = pl.ds(base + 3 * ROWS, half)
            even = oback[2 * m, r, :].astype(F32)
            odd = oback[2 * m + 1, r, :].astype(F32)
            oall[pl.ds(i * ROWS, half), pl.ds(col + 384, TOK)] = (
                jnp.where(low_lanes, even, odd).astype(BF))
            oall[pl.ds(i * ROWS + half, half), pl.ds(col + 384, TOK)] = (
                pltpu.roll(jnp.where(low_lanes, odd, even), 64, 1).astype(BF))

    def bounds():
        for d in range(1, 8):
            at = bnd.at[m8(y - d)]
            remote(at, at, s_b.at[d - 1], r_b.at[d - 1], on_line(y + d)).wait_recv()

    def tokens_in(i):
        for k in (0, 4, 5, 6):
            tok_arrived(i, k)

    def partial_out(i):
        partial(i)
        p_start(i, range(4))

    def pass_weights(n):
        for k in (0, 1):
            w_wait(n, (k,))
            w_start(n, (k + 2,))

    def from_other_core():
        remote(tok, toks, s_sib.at[0], r_sib.at[0], (other, place)).wait_recv()
        remote(dmine, dests, s_sib.at[1], r_sib.at[1], (other, place)).wait_recv()
        remote(smine, scos, s_sib.at[2], r_sib.at[2], (other, place)).wait_recv()

    work = dict(
        F=forward, D=own_weights, B=bounds, T=tokens_in, W=pass_weights, V=w_start,
        X=w_wait, P=partial_out, R=relayed, H=hidden, G=pass_on, O=expert_out,
        S=from_other_core, C=collect)
    for step in ORDER:
        work[step[0]](*step[1:])

    back = onehot(dests[...] == lane.astype(F32)).astype(BF)

    @pl.loop(0, 7)
    def _(c):
        at = pl.ds(pl.multiple_of(c * 512, 512), 512)
        gain = scos[...]
        moved = dot(back, oall[:, at])
        gain = jnp.concatenate([gain] * 4, axis=1)
        out[:, at] = (toks[:, at].astype(F32) + gain * moved).astype(BF)

    for copy in pending:
        copy.wait_send()


def body(tokens, routing, scores, w_gate, w_up, w_down):
    vmem = pl.BlockSpec(memory_space=pltpu.VMEM)
    hbm = pl.BlockSpec(memory_space=pl.ANY)
    dma = pltpu.SemaphoreType.DMA
    result = pl.pallas_call(
        kernel,
        out_shape=jax.ShapeDtypeStruct((TOK, D), BF),
        in_specs=[vmem, vmem, vmem, hbm, hbm, hbm],
        out_specs=vmem,
        scratch_shapes=[
            pltpu.VMEM((4, TOK, QD), BF),
            pltpu.VMEM((8, TOK, QD), BF),
            pltpu.VMEM((8, 8, TOK), F32),
            pltpu.VMEM((8, TOK, 2 * HB), F32),
            pltpu.VMEM((8, TOK, 2 * HB), BF),
            pltpu.VMEM((2, TOK, 2 * HB), BF),
            pltpu.VMEM((2, 2, TOK, 2 * HB), BF),
            pltpu.VMEM((2, 8, TOK, HB), BF),
            pltpu.VMEM((3, 8 * ROWS, QD), BF),
            pltpu.VMEM((3, 8 * ROWS, 2 * HB), BF),
            pltpu.VMEM((4, 2, QD, HB), BF),
            pltpu.VMEM((4, 448, 2 * HB), BF),
            pltpu.VMEM((8, STAGES * FOLD, TOK), BF),
            pltpu.VMEM((8, STAGES * FOLD, TOK), BF),
            pltpu.VMEM((TOK, D), BF),
            pltpu.VMEM((TOK, TOK), F32),
            pltpu.VMEM((TOK, TOK), F32),
            pltpu.VMEM((TOK, TOK), F32),
            pltpu.VMEM((TOK, TOK), F32),
            pltpu.VMEM((TOK, D), BF),
            dma((3,)),
            dma((3, 4)), dma((3, 4)),
            dma((7,)), dma((7,)),
            dma((3,)), dma((3,)),
            dma((STAGES, 7)), dma((STAGES, 7)),
            dma((STAGES, 6)), dma((STAGES, 6)),
            dma((STAGES, 4, 2)), dma((STAGES, 4, 2)),
            dma((STAGES, 8)), dma((STAGES, 8)),
        ],
        compiler_params=pltpu.CompilerParams(
            collective_id=0, has_side_effects=True, vmem_limit_bytes=52 * 2**20),
        cost_estimate=pl.CostEstimate(
            flops=8 * 10**9, bytes_accessed=6 * 10**6, transcendentals=131072),
    )(tokens[0], routing[0], scores[0], w_gate[0, 0], w_up[0, 0], w_down[0, 0].T)
    return result[None]


def solution(mesh):
    return jax.shard_map(
        body,
        mesh=mesh,
        in_specs=(
            P("pipe", "expert", None),
            P("pipe", "expert", None),
            P("pipe", "expert", None),
            P("pipe", "expert", None, None),
            P("pipe", "expert", None, None),
            P("pipe", "expert", None, None),
        ),
        out_specs=P("pipe", "expert", None),
        check_vma=False,
    )
```

```python
import functools
import jax
import jax.numpy as jnp
from jax import lax
from jax.experimental import pallas as pl
from jax.experimental.pallas import tpu as pltpu
from jax.sharding import PartitionSpec as P

MESH = pl.DeviceIdType.MESH
BF = jnp.bfloat16
F32 = jnp.float32

D = 3584
TOK = 128
QD = 896
HB = 512
STAGES = 4
ROWS = TOK // STAGES
FOLD = ROWS * 7 // 2
NEEDS = ((0, 1), (0, 1, 2), (1, 2, 3), (2, 3))
ORDER = (
    ("F", 0), ("D",), ("B",), ("F", 1), ("F", 2), ("W", 0), ("W", 1), ("F", 3),
    ("T", 0), ("T", 1), ("P", 0, 0), ("T", 2), ("P", 1, 0), ("T", 3),
    ("W", 2), ("W", 3), ("V", 4, (0, 1)),
    ("P", 0, 1), ("R", 0, 0), ("P", 1, 1), ("R", 1, 0), ("R", 0, 1),
    ("X", 0, (2, 3)), ("X", 1, (2, 3)), ("P", 2, 0), ("R", 1, 1),
    ("P", 3, 0), ("H", 0), ("G", 0, 2), ("R", 2, 0), ("H", 1), ("G", 0, 3), ("G", 1, 2),
    ("X", 2, (2, 3)), ("X", 3, (2, 3)), ("P", 2, 1), ("R", 3, 0), ("P", 3, 1),
    ("G", 0, 4), ("G", 1, 3), ("R", 2, 1), ("G", 1, 4), ("R", 3, 1),
    ("H", 2), ("G", 2, 2), ("H", 3), ("G", 2, 3), ("G", 3, 2), ("W", 4),
    ("O", 0), ("G", 2, 4), ("G", 3, 3), ("O", 1), ("G", 3, 4),
    ("X", 4, (2, 3)), ("O", 2), ("O", 3),
    ("S",), ("C", 0), ("C", 1), ("C", 2), ("C", 3),
)


def dot(a, b):
    return jnp.dot(a, b, preferred_element_type=F32)


def iota(shape, axis):
    return lax.broadcasted_iota(jnp.int32, shape, axis)


def onehot(cond):
    return jnp.where(cond, 1.0, 0.0).astype(F32)


def kernel(tok, routing, scores, w_gate, w_up, w_down, out,
           rq, xa, bnd, part, psend, relay, near, hid, lhs, lhd, wgu, wd,
           osend, oback, toks, dests, scos, dmine, smine, oall,
           s_loc, s_w, r_w, s_b, r_b, s_sib, r_sib, s_tok, r_tok, s_p, r_p,
           s_h, r_h, s_o, r_o):
    pipe = lax.axis_index("pipe")
    place = lax.axis_index("expert")
    x, y = place // 8, place % 8
    a, b = y // 2, y % 2
    sig = 1 - 2 * b
    other = pipe + 1 - 2 * (pipe % 2)

    def m8(v):
        return lax.rem(v + 16, 8)

    def on_line(v):
        return (pipe, x * 8 + m8(v))

    def on_cross(v):
        return (pipe, lax.rem(x + v + 4, 4) * 8 + y)

    barrier = pltpu.get_barrier_semaphore()
    for d in range(1, 8):
        pl.semaphore_signal(barrier, inc=1, device_id=on_line(y + d), device_id_type=MESH)
    for d in range(1, 4):
        pl.semaphore_signal(barrier, inc=1, device_id=on_cross(d), device_id_type=MESH)
    for d in range(8):
        pl.semaphore_signal(barrier, inc=1, device_id=(other, x * 8 + d), device_id_type=MESH)

    pending = []

    def remote(src, dst, ssem, rsem, device):
        return pltpu.make_async_remote_copy(
            src_ref=src, dst_ref=dst, send_sem=ssem, recv_sem=rsem,
            device_id=device, device_id_type=MESH)

    def send(*args):
        copy = remote(*args)
        copy.start()
        pending.append(copy)
        return copy

    def w_own(n):
        if n == 4:
            return w_down
        return (w_gate, w_up)[n % 2].at[:, pl.ds(n // 2 * 256, 256)]

    def w_held(n, slot):
        return wd.at[slot] if n == 4 else wgu.at[slot, n // 2, n % 2]

    local = []
    for n in range(5):
        copy = pltpu.make_async_copy(w_own(n), w_held(n, 0), s_loc.at[n])
        copy.start()
        local.append(copy)

    rel = lax.rem(routing[...] - x + 4, 4)
    key = jnp.where(rel == 2, 3, jnp.where(rel == 3, 2, rel))
    lane = iota((TOK, TOK), 1)
    sub = iota((TOK, TOK), 0)
    member = onehot(key == lane)
    member16 = member.astype(BF)
    before = dot(onehot(lane < sub).astype(BF), member16)
    total = dot(jnp.ones((TOK, TOK), BF), member16)
    start = dot(total.astype(BF), onehot(sub < lane).astype(BF))
    dest = jnp.sum((start + before) * member, axis=1, keepdims=True)
    dest = jnp.broadcast_to(dest, (TOK, TOK))
    dmine[...] = dest
    smine[...] = jnp.broadcast_to(scores[...], (TOK, TOK))
    first = jnp.sum(
        jnp.where(lane[:8] == sub[:8], start[:8], 0.0), axis=1, keepdims=True)
    bnd[y] = jnp.broadcast_to(first, (8, TOK))
    place_of = onehot(dest == lane.astype(F32)).T.astype(BF)

    pl.semaphore_wait(barrier, 18)

    def w_copy(n, k):
        own = w_own(n)
        held = [None] + [w_held(n, slot) for slot in (1, 2, 3)]
        size = 224 if n == 4 else QD // 2
        halves = (pl.ds(0, size), pl.ds(size, size))
        src = (own, own, held[1].at[halves[0]], held[2].at[halves[1]])[k]
        dst = (held[1], held[2], held[3].at[halves[0]], held[3].at[halves[1]])[k]
        return remote(src, dst, s_w.at[n, k], r_w.at[n, k], on_cross((-1, 1, -1, 1)[k]))

    def w_start(n, ks):
        for k in ks:
            copy = w_copy(n, k)
            copy.start()
            pending.append(copy)

    def w_wait(n, ks):
        for k in ks:
            w_copy(n, k).wait_recv()

    for n in range(4):
        w_start(n, (0, 1))

    kinds = (sig, 2 * sig, -sig, -3 * sig)
    sources = [m8(y + v) for v in
               (sig, -2 * sig, -sig, -3 * sig, 3 * sig, 2 * sig, 4 * sig)]

    for d in range(1, 8):
        send(bnd.at[y], bnd.at[y], s_b.at[d - 1], r_b.at[d - 1], on_line(y + d))

    for i in range(STAGES):
        rows = pl.ds(i * ROWS, ROWS)
        for q in range(4):
            rq[q, rows, :] = dot(
                place_of[i * ROWS:(i + 1) * ROWS], tok[:, q * QD:(q + 1) * QD]).astype(BF)
        for k in (3, 1, 2, 0):
            to = m8(y + kinds[k])
            send(rq.at[to // 2, rows], xa.at[y, rows],
                 s_tok.at[i, k], r_tok.at[i, k], on_line(to))
        xa[y, rows, :] = rq[a, rows, :]

    send(tok, toks, s_sib.at[0], r_sib.at[0], (other, place))
    send(dmine, dests, s_sib.at[1], r_sib.at[1], (other, place))
    send(smine, scos, s_sib.at[2], r_sib.at[2], (other, place))

    def tok_arrived(i, k):
        at = xa.at[sources[k], pl.ds(i * ROWS, ROWS)]
        remote(at, at, s_tok.at[i, k], r_tok.at[i, k], on_line(y + 1)).wait_recv()
        return at

    def forward(i):
        for k in (2, 1, 3):
            at = tok_arrived(i, k)
            send(at, at, s_tok.at[i, k + 3], r_tok.at[i, k + 3], on_line(y + sig))

    def own_weights():
        for copy in local:
            copy.wait()

    def mask(s, i, j):
        row = iota((ROWS, TOK), 0).astype(F32) + float(i * ROWS)
        low = bnd[s, j:j + 1, :]
        high = bnd[s, j + 1:j + 2, :]
        return onehot((row >= low) & (row < high)).astype(BF)

    def masked_tokens(i):
        rows = pl.ds(i * ROWS, ROWS)
        for n, j in enumerate(NEEDS[i]):
            @pl.loop(0, 8)
            def _(s):
                m = mask(s, i, j)
                at = pl.ds(pl.multiple_of(s * ROWS, ROWS), ROWS)
                for c in range(7):
                    lanes = pl.ds(c * TOK, TOK)
                    lhs[i, n, at, lanes] = xa[s, rows, lanes] * m

    def partial(i, c):
        rows = pl.ds(i * ROWS, ROWS)

        @pl.loop(0, 2)
        def _(h):
            acc = sum(dot(lhs[i, n], wgu[j, c, h]) for n, j in enumerate(NEEDS[i]))
            acc = acc.reshape(8, ROWS, 256)
            col = pl.ds(pl.multiple_of(c * HB + h * 256, 256), 256)
            part[:, rows, col] = acc
            psend[:, rows, col] = acc.astype(BF)

    far = 2 * lax.rem(a + 2, 4)
    up = 2 * lax.rem(a + 1, 4)
    down = 2 * lax.rem(a + 3, 4)

    def p_copy(i, c, k):
        rows = pl.ds(i * ROWS, ROWS)
        cols = pl.ds(c * HB, HB)
        src = (far, far + 1, up + 1, down, up, down + 1)[k]
        dst = (relay.at[0, rows, cols], relay.at[1, rows, cols],
               near.at[0, 1, rows, cols], near.at[1, 0, rows, cols],
               near.at[0, 0, rows, cols], near.at[1, 1, rows, cols])[k]
        to = (2, -2, 2, -2, 2, -2)[k]
        return remote(psend.at[src, rows, cols], dst, s_p.at[i, c, k], r_p.at[i, c, k],
                      on_line(y + to))

    def p_start(i, c, ks):
        for k in ks:
            copy = p_copy(i, c, k)
            copy.start()
            pending.append(copy)

    def relayed(i, c):
        rows = pl.ds(i * ROWS, ROWS)
        cols = pl.ds(c * HB, HB)
        for k, s in ((0, up), (1, down + 1)):
            p_copy(i, c, k).wait_recv()
            psend[s, rows, cols] = (
                part[s, rows, cols] + relay[k, rows, cols].astype(F32)).astype(BF)
            p_start(i, c, (k + 4,))

    def h_copy(i, t, way):
        step = (1, -1)[way]
        owner = m8(y - step * (t - 1))
        rows = pl.ds(i * ROWS, ROWS)
        src = 2 * (owner // 2)
        if t == 4:
            at = hid.at[owner % 2, pl.ds(src + way, 1), rows]
        else:
            at = hid.at[owner % 2, pl.ds(src, 2), rows]
        return remote(at, at, s_h.at[i, t - 1, way], r_h.at[i, t - 1, way], on_line(y + step))

    def h_start(i, t):
        for way in (0, 1):
            copy = h_copy(i, t, way)
            copy.start()
            pending.append(copy)

    def h_arrived(i, t):
        for way in (0, 1):
            step = (1, -1)[way]
            owner = m8(y - step * t)
            rows = pl.ds(i * ROWS, ROWS)
            src = 2 * (owner // 2)
            if t == 4:
                at = hid.at[owner % 2, pl.ds(src + way, 1), rows]
            else:
                at = hid.at[owner % 2, pl.ds(src, 2), rows]
            remote(at, at, s_h.at[i, t - 1, way], r_h.at[i, t - 1, way],
                   on_line(y + step)).wait_recv()

    def hidden(i):
        rows = pl.ds(i * ROWS, ROWS)
        for c in (0, 1):
            for k in (2, 3, 4, 5):
                p_copy(i, c, k).wait_recv()
        for c in (0, 1):
            cols = pl.ds(c * HB, HB)
            for k in (0, 1):
                s = 2 * a + k
                whole = (part[s, rows, cols] + near[0, k, rows, cols].astype(F32)
                         + near[1, k, rows, cols].astype(F32))
                g, u = whole[:, :256], whole[:, 256:]
                hid[b, s, rows, pl.ds(c * 256, 256)] = (
                    g / (1.0 + jnp.exp(-g)) * u).astype(BF)
        h_start(i, 1)

    def pass_on(i, t):
        h_arrived(i, t - 1)
        h_start(i, t)

    def expert_out(i):
        h_arrived(i, 4)
        rows = pl.ds(i * ROWS, ROWS)
        for n, j in enumerate(NEEDS[i]):
            @pl.loop(0, 8)
            def _(s):
                m = mask(s, i, j)
                at = pl.ds(pl.multiple_of(s * ROWS, ROWS), ROWS)
                for c in range(8):
                    lhd[n, at, pl.ds(c * TOK, TOK)] = (
                        hid[c // 4, s, rows, pl.ds((c % 4) * TOK, TOK)] * m)

        keep = iota((16, TOK), 1) // 64 == b
        half = ROWS // 2
        base = i * FOLD

        def term(n, cols):
            return lax.dot_general(
                lhd[n], cols, (((1,), (1,)), ((), ())), preferred_element_type=F32)

        @pl.loop(0, 3)
        def _(c):
            at = pl.ds(pl.multiple_of(c * TOK + 64 * b, 64), TOK)
            acc = sum(term(n, wd[j, at, :]) for n, j in enumerate(NEEDS[i]))
            low = pl.multiple_of(base + c * ROWS, 16)
            osend[:, pl.ds(low, ROWS), :] = acc.reshape(8, ROWS, TOK).astype(BF)

        at = pl.ds(pl.multiple_of(384 * (1 - b), 64), 64)
        acc = 0.0
        for n, j in enumerate(NEEDS[i]):
            rest = wd[j, at, :]
            acc = acc + term(n, jnp.concatenate([rest, rest], axis=0))
        acc = acc.reshape(8, ROWS, TOK)
        folded = jnp.where(keep[None], acc[:, :half], acc[:, half:])
        osend[:, pl.ds(base + 3 * ROWS, half), :] = folded.astype(BF)

        fold = pl.ds(base, FOLD)
        for d in (4, 3, 5, 2, 6, 1, 7, 0):
            to = m8(y + d)
            send(osend.at[to, fold], oback.at[y, fold],
                 s_o.at[i, d], r_o.at[i, d], (other, x * 8 + to))

    def collect(i):
        base = i * FOLD
        fold = pl.ds(base, FOLD)
        for d in range(8):
            at = oback.at[m8(y - d), fold]
            remote(at, at, s_o.at[i, d], r_o.at[i, d], (other, place)).wait_recv()
        half = ROWS // 2
        low_lanes = iota((half, TOK), 1) < 64
        for m in range(4):
            col = m * QD
            for c in range(3):
                r = pl.ds(base + c * ROWS, ROWS)
                oall[pl.ds(i * ROWS, ROWS), pl.ds(col + c * TOK, TOK)] = oback[2 * m, r, :]
                oall[pl.ds(i * ROWS, ROWS), pl.ds(col + 512 + c * TOK, TOK)] = (
                    oback[2 * m + 1, r, :])
            r = pl.ds(base + 3 * ROWS, half)
            even = oback[2 * m, r, :].astype(F32)
            odd = oback[2 * m + 1, r, :].astype(F32)
            oall[pl.ds(i * ROWS, half), pl.ds(col + 384, TOK)] = (
                jnp.where(low_lanes, even, odd).astype(BF))
            oall[pl.ds(i * ROWS + half, half), pl.ds(col + 384, TOK)] = (
                pltpu.roll(jnp.where(low_lanes, odd, even), 64, 1).astype(BF))

    def bounds():
        for d in range(1, 8):
            at = bnd.at[m8(y - d)]
            remote(at, at, s_b.at[d - 1], r_b.at[d - 1], on_line(y + d)).wait_recv()

    def tokens_in(i):
        for k in (0, 4, 5, 6):
            tok_arrived(i, k)

    def partial_out(i, c):
        if c == 0:
            masked_tokens(i)
        partial(i, c)
        p_start(i, c, range(4))

    def pass_weights(n):
        for k in (0, 1):
            w_wait(n, (k,))
            w_start(n, (k + 2,))

    def from_other_core():
        remote(tok, toks, s_sib.at[0], r_sib.at[0], (other, place)).wait_recv()
        remote(dmine, dests, s_sib.at[1], r_sib.at[1], (other, place)).wait_recv()
        remote(smine, scos, s_sib.at[2], r_sib.at[2], (other, place)).wait_recv()

    work = dict(
        F=forward, D=own_weights, B=bounds, T=tokens_in, W=pass_weights, V=w_start,
        X=w_wait, P=partial_out, R=relayed, H=hidden, G=pass_on, O=expert_out,
        S=from_other_core, C=collect)
    for step in ORDER:
        work[step[0]](*step[1:])

    back = onehot(dests[...] == lane.astype(F32)).astype(BF)

    @pl.loop(0, 7)
    def _(c):
        at = pl.ds(pl.multiple_of(c * 512, 512), 512)
        gain = scos[...]
        moved = dot(back, oall[:, at])
        gain = jnp.concatenate([gain] * 4, axis=1)
        out[:, at] = (toks[:, at].astype(F32) + gain * moved).astype(BF)

    for copy in pending:
        copy.wait_send()


def body(tokens, routing, scores, w_gate, w_up, w_down):
    vmem = pl.BlockSpec(memory_space=pltpu.VMEM)
    hbm = pl.BlockSpec(memory_space=pl.ANY)
    dma = pltpu.SemaphoreType.DMA
    result = pl.pallas_call(
        kernel,
        out_shape=jax.ShapeDtypeStruct((TOK, D), BF),
        in_specs=[vmem, vmem, vmem, hbm, hbm, hbm],
        out_specs=vmem,
        scratch_shapes=[
            pltpu.VMEM((4, TOK, QD), BF),
            pltpu.VMEM((8, TOK, QD), BF),
            pltpu.VMEM((8, 8, TOK), F32),
            pltpu.VMEM((8, TOK, 2 * HB), F32),
            pltpu.VMEM((8, TOK, 2 * HB), BF),
            pltpu.VMEM((2, TOK, 2 * HB), BF),
            pltpu.VMEM((2, 2, TOK, 2 * HB), BF),
            pltpu.VMEM((2, 8, TOK, HB), BF),
            pltpu.VMEM((STAGES, 3, 8 * ROWS, QD), BF),
            pltpu.VMEM((3, 8 * ROWS, 2 * HB), BF),
            pltpu.VMEM((4, 2, 2, QD, 256), BF),
            pltpu.VMEM((4, 448, 2 * HB), BF),
            pltpu.VMEM((8, STAGES * FOLD, TOK), BF),
            pltpu.VMEM((8, STAGES * FOLD, TOK), BF),
            pltpu.VMEM((TOK, D), BF),
            pltpu.VMEM((TOK, TOK), F32),
            pltpu.VMEM((TOK, TOK), F32),
            pltpu.VMEM((TOK, TOK), F32),
            pltpu.VMEM((TOK, TOK), F32),
            pltpu.VMEM((TOK, D), BF),
            dma((5,)),
            dma((5, 4)), dma((5, 4)),
            dma((7,)), dma((7,)),
            dma((3,)), dma((3,)),
            dma((STAGES, 7)), dma((STAGES, 7)),
            dma((STAGES, 2, 6)), dma((STAGES, 2, 6)),
            dma((STAGES, 4, 2)), dma((STAGES, 4, 2)),
            dma((STAGES, 8)), dma((STAGES, 8)),
        ],
        compiler_params=pltpu.CompilerParams(
            collective_id=0, has_side_effects=True, vmem_limit_bytes=52 * 2**20),
        cost_estimate=pl.CostEstimate(
            flops=8 * 10**9, bytes_accessed=6 * 10**6, transcendentals=131072),
    )(tokens[0], routing[0], scores[0], w_gate[0, 0], w_up[0, 0], w_down[0, 0].T)
    return result[None]


def solution(mesh):
    return jax.shard_map(
        body,
        mesh=mesh,
        in_specs=(
            P("pipe", "expert", None),
            P("pipe", "expert", None),
            P("pipe", "expert", None),
            P("pipe", "expert", None, None),
            P("pipe", "expert", None, None),
            P("pipe", "expert", None, None),
        ),
        out_specs=P("pipe", "expert", None),
        check_vma=False,
    )
```

```python
import functools
import jax
import jax.numpy as jnp
from jax import lax
from jax.experimental import pallas as pl
from jax.experimental.pallas import tpu as pltpu
from jax.sharding import PartitionSpec as P

MESH = pl.DeviceIdType.MESH
BF = jnp.bfloat16
F32 = jnp.float32

D = 3584
TOK = 128
QD = 896
HB = 512
STAGES = 4
ROWS = TOK // STAGES
FOLD = ROWS * 7 // 2
NEEDS = ((0, 1), (0, 1, 2), (1, 2, 3), (2, 3))
ORDER = (
    ("F", 0), ("D",), ("B",), ("F", 1), ("F", 2), ("W", 0), ("W", 1), ("F", 3), ("T", 0),
    ("T", 1), ("P", 0, 0), ("T", 2), ("P", 1, 0), ("T", 3), ("W", 2), ("W", 3),
    ("V", 4, (0, 1)), ("P", 0, 1), ("R", 0, 0), ("P", 1, 1), ("R", 1, 0), ("R", 0, 1),
    ("X", 0, (2, 3)), ("X", 1, (2, 3)), ("P", 2, 0), ("R", 1, 1), ("P", 3, 0), ("H", 0),
    ("G", 0, 2), ("R", 2, 0), ("H", 1), ("G", 0, 3), ("G", 1, 2), ("X", 2, (2, 3)),
    ("X", 3, (2, 3)), ("P", 2, 1), ("R", 3, 0), ("P", 3, 1), ("G", 0, 4), ("G", 1, 3),
    ("R", 2, 1), ("G", 1, 4), ("R", 3, 1), ("H", 2), ("G", 2, 2), ("H", 3), ("G", 2, 3),
    ("G", 3, 2), ("W", 4), ("O", 0), ("O", 1), ("G", 3, 3), ("G", 2, 4), ("X", 4, (2, 3)),
    ("G", 3, 4), ("O", 2), ("O", 3), ("S",), ("C", 0), ("C", 1), ("C", 2), ("C", 3),
)


def dot(a, b):
    return jnp.dot(a, b, preferred_element_type=F32)


def iota(shape, axis):
    return lax.broadcasted_iota(jnp.int32, shape, axis)


def onehot(cond):
    return jnp.where(cond, 1.0, 0.0).astype(F32)


def kernel(tok, routing, scores, w_gate, w_up, w_down, out,
           rq, xa, bnd, part, psend, relay, near, hid, lhs, lhd, wgu, wd,
           osend, oback, toks, dests, scos, dmine, smine, oall,
           s_loc, s_w, r_w, s_b, r_b, s_sib, r_sib, s_tok, r_tok, s_p, r_p,
           s_h, r_h, s_o, r_o):
    pipe = lax.axis_index("pipe")
    place = lax.axis_index("expert")
    x, y = place // 8, place % 8
    a, b = y // 2, y % 2
    sig = 1 - 2 * b
    other = pipe + 1 - 2 * (pipe % 2)

    def m8(v):
        return lax.rem(v + 16, 8)

    def on_line(v):
        return (pipe, x * 8 + m8(v))

    def on_cross(v):
        return (pipe, lax.rem(x + v + 4, 4) * 8 + y)

    barrier = pltpu.get_barrier_semaphore()
    for d in range(1, 8):
        pl.semaphore_signal(barrier, inc=1, device_id=on_line(y + d), device_id_type=MESH)
    for d in range(1, 4):
        pl.semaphore_signal(barrier, inc=1, device_id=on_cross(d), device_id_type=MESH)
    for d in range(8):
        pl.semaphore_signal(barrier, inc=1, device_id=(other, x * 8 + d), device_id_type=MESH)

    pending = []

    def remote(src, dst, ssem, rsem, device):
        return pltpu.make_async_remote_copy(
            src_ref=src, dst_ref=dst, send_sem=ssem, recv_sem=rsem,
            device_id=device, device_id_type=MESH)

    def send(*args):
        copy = remote(*args)
        copy.start()
        pending.append(copy)
        return copy

    def w_own(n):
        if n == 4:
            return w_down
        return (w_gate, w_up)[n % 2].at[:, pl.ds(n // 2 * 256, 256)]

    def w_held(n, slot):
        return wd.at[slot] if n == 4 else wgu.at[slot, n // 2, n % 2]

    local = []
    for n in range(5):
        copy = pltpu.make_async_copy(w_own(n), w_held(n, 0), s_loc.at[n])
        copy.start()
        local.append(copy)

    rel = lax.rem(routing[...] - x + 4, 4)
    key = jnp.where(rel == 2, 3, jnp.where(rel == 3, 2, rel))
    lane = iota((TOK, TOK), 1)
    sub = iota((TOK, TOK), 0)
    member = onehot(key == lane)
    member16 = member.astype(BF)
    before = dot(onehot(lane < sub).astype(BF), member16)
    total = dot(jnp.ones((TOK, TOK), BF), member16)
    start = dot(total.astype(BF), onehot(sub < lane).astype(BF))
    dest = jnp.sum((start + before) * member, axis=1, keepdims=True)
    dest = jnp.broadcast_to(dest, (TOK, TOK))
    dmine[...] = dest
    smine[...] = jnp.broadcast_to(scores[...], (TOK, TOK))
    first = jnp.sum(
        jnp.where(lane[:8] == sub[:8], start[:8], 0.0), axis=1, keepdims=True)
    bnd[y] = jnp.broadcast_to(first, (8, TOK))
    place_of = onehot(dest == lane.astype(F32)).T.astype(BF)

    pl.semaphore_wait(barrier, 18)

    def w_copy(n, k):
        own = w_own(n)
        held = [None] + [w_held(n, slot) for slot in (1, 2, 3)]
        size = 224 if n == 4 else QD // 2
        halves = (pl.ds(0, size), pl.ds(size, size))
        src = (own, own, held[1].at[halves[0]], held[2].at[halves[1]])[k]
        dst = (held[1], held[2], held[3].at[halves[0]], held[3].at[halves[1]])[k]
        return remote(src, dst, s_w.at[n, k], r_w.at[n, k], on_cross((-1, 1, -1, 1)[k]))

    def w_start(n, ks):
        for k in ks:
            copy = w_copy(n, k)
            copy.start()
            pending.append(copy)

    def w_wait(n, ks):
        for k in ks:
            w_copy(n, k).wait_recv()

    for n in range(4):
        w_start(n, (0, 1))

    kinds = (sig, 2 * sig, -sig, -3 * sig)
    sources = [m8(y + v) for v in
               (sig, -2 * sig, -sig, -3 * sig, 3 * sig, 2 * sig, 4 * sig)]

    for d in range(1, 8):
        send(bnd.at[y], bnd.at[y], s_b.at[d - 1], r_b.at[d - 1], on_line(y + d))

    for i in range(STAGES):
        rows = pl.ds(i * ROWS, ROWS)
        for q in range(4):
            rq[q, rows, :] = dot(
                place_of[i * ROWS:(i + 1) * ROWS], tok[:, q * QD:(q + 1) * QD]).astype(BF)
        for k in (3, 1, 2, 0):
            to = m8(y + kinds[k])
            send(rq.at[to // 2, rows], xa.at[y, rows],
                 s_tok.at[i, k], r_tok.at[i, k], on_line(to))
        xa[y, rows, :] = rq[a, rows, :]

    send(tok, toks, s_sib.at[0], r_sib.at[0], (other, place))
    send(dmine, dests, s_sib.at[1], r_sib.at[1], (other, place))
    send(smine, scos, s_sib.at[2], r_sib.at[2], (other, place))

    def tok_arrived(i, k):
        at = xa.at[sources[k], pl.ds(i * ROWS, ROWS)]
        remote(at, at, s_tok.at[i, k], r_tok.at[i, k], on_line(y + 1)).wait_recv()
        return at

    def forward(i):
        for k in (2, 1, 3):
            at = tok_arrived(i, k)
            send(at, at, s_tok.at[i, k + 3], r_tok.at[i, k + 3], on_line(y + sig))

    def own_weights():
        for copy in local:
            copy.wait()

    def mask(s, i, j):
        row = iota((ROWS, TOK), 0).astype(F32) + float(i * ROWS)
        low = bnd[s, j:j + 1, :]
        high = bnd[s, j + 1:j + 2, :]
        return onehot((row >= low) & (row < high)).astype(BF)

    def masked_tokens(i):
        rows = pl.ds(i * ROWS, ROWS)
        for n, j in enumerate(NEEDS[i]):
            @pl.loop(0, 8)
            def _(s):
                m = mask(s, i, j)
                at = pl.ds(pl.multiple_of(s * ROWS, ROWS), ROWS)
                for c in range(7):
                    lanes = pl.ds(c * TOK, TOK)
                    lhs[i, n, at, lanes] = xa[s, rows, lanes] * m

    def partial(i, c):
        rows = pl.ds(i * ROWS, ROWS)

        @pl.loop(0, 2)
        def _(h):
            acc = sum(dot(lhs[i, n], wgu[j, c, h]) for n, j in enumerate(NEEDS[i]))
            acc = acc.reshape(8, ROWS, 256)
            col = pl.ds(pl.multiple_of(c * HB + h * 256, 256), 256)
            part[:, rows, col] = acc
            psend[:, rows, col] = acc.astype(BF)

    far = 2 * lax.rem(a + 2, 4)
    up = 2 * lax.rem(a + 1, 4)
    down = 2 * lax.rem(a + 3, 4)

    def p_copy(i, c, k):
        rows = pl.ds(i * ROWS, ROWS)
        cols = pl.ds(c * HB, HB)
        src = (far, far + 1, up + 1, down, up, down + 1)[k]
        dst = (relay.at[0, rows, cols], relay.at[1, rows, cols],
               near.at[0, 1, rows, cols], near.at[1, 0, rows, cols],
               near.at[0, 0, rows, cols], near.at[1, 1, rows, cols])[k]
        to = (2, -2, 2, -2, 2, -2)[k]
        return remote(psend.at[src, rows, cols], dst, s_p.at[i, c, k], r_p.at[i, c, k],
                      on_line(y + to))

    def p_start(i, c, ks):
        for k in ks:
            copy = p_copy(i, c, k)
            copy.start()
            pending.append(copy)

    def relayed(i, c):
        rows = pl.ds(i * ROWS, ROWS)
        cols = pl.ds(c * HB, HB)
        for k, s in ((0, up), (1, down + 1)):
            p_copy(i, c, k).wait_recv()
            psend[s, rows, cols] = (
                part[s, rows, cols] + relay[k, rows, cols].astype(F32)).astype(BF)
            p_start(i, c, (k + 4,))

    def h_copy(i, t, way):
        step = (1, -1)[way]
        owner = m8(y - step * (t - 1))
        rows = pl.ds(i * ROWS, ROWS)
        src = 2 * (owner // 2)
        if t == 4:
            at = hid.at[owner % 2, pl.ds(src + way, 1), rows]
        else:
            at = hid.at[owner % 2, pl.ds(src, 2), rows]
        return remote(at, at, s_h.at[i, t - 1, way], r_h.at[i, t - 1, way], on_line(y + step))

    def h_start(i, t):
        for way in (0, 1):
            copy = h_copy(i, t, way)
            copy.start()
            pending.append(copy)

    def h_arrived(i, t):
        for way in (0, 1):
            step = (1, -1)[way]
            owner = m8(y - step * t)
            rows = pl.ds(i * ROWS, ROWS)
            src = 2 * (owner // 2)
            if t == 4:
                at = hid.at[owner % 2, pl.ds(src + way, 1), rows]
            else:
                at = hid.at[owner % 2, pl.ds(src, 2), rows]
            remote(at, at, s_h.at[i, t - 1, way], r_h.at[i, t - 1, way],
                   on_line(y + step)).wait_recv()

    def hidden(i):
        rows = pl.ds(i * ROWS, ROWS)
        for c in (0, 1):
            for k in (2, 3, 4, 5):
                p_copy(i, c, k).wait_recv()
        for c in (0, 1):
            cols = pl.ds(c * HB, HB)
            for k in (0, 1):
                s = 2 * a + k
                whole = (part[s, rows, cols] + near[0, k, rows, cols].astype(F32)
                         + near[1, k, rows, cols].astype(F32))
                g, u = whole[:, :256], whole[:, 256:]
                hid[b, s, rows, pl.ds(c * 256, 256)] = (
                    g / (1.0 + jnp.exp(-g)) * u).astype(BF)
        h_start(i, 1)

    def pass_on(i, t):
        h_arrived(i, t - 1)
        h_start(i, t)

    def expert_out(i):
        h_arrived(i, 4)
        rows = pl.ds(i * ROWS, ROWS)
        for n, j in enumerate(NEEDS[i]):
            @pl.loop(0, 8)
            def _(s):
                m = mask(s, i, j)
                at = pl.ds(pl.multiple_of(s * ROWS, ROWS), ROWS)
                for c in range(8):
                    lhd[n, at, pl.ds(c * TOK, TOK)] = (
                        hid[c // 4, s, rows, pl.ds((c % 4) * TOK, TOK)] * m)

        keep = iota((16, TOK), 1) // 64 == b
        half = ROWS // 2
        base = i * FOLD

        def term(n, cols):
            return lax.dot_general(
                lhd[n], cols, (((1,), (1,)), ((), ())), preferred_element_type=F32)

        @pl.loop(0, 3)
        def _(c):
            at = pl.ds(pl.multiple_of(c * TOK + 64 * b, 64), TOK)
            acc = sum(term(n, wd[j, at, :]) for n, j in enumerate(NEEDS[i]))
            low = pl.multiple_of(base + c * ROWS, 16)
            osend[:, pl.ds(low, ROWS), :] = acc.reshape(8, ROWS, TOK).astype(BF)

        at = pl.ds(pl.multiple_of(384 * (1 - b), 64), 64)
        acc = 0.0
        for n, j in enumerate(NEEDS[i]):
            rest = wd[j, at, :]
            acc = acc + term(n, jnp.concatenate([rest, rest], axis=0))
        acc = acc.reshape(8, ROWS, TOK)
        folded = jnp.where(keep[None], acc[:, :half], acc[:, half:])
        osend[:, pl.ds(base + 3 * ROWS, half), :] = folded.astype(BF)

        fold = pl.ds(base, FOLD)
        for d in (4, 3, 5, 2, 6, 1, 7, 0):
            to = m8(y + d)
            send(osend.at[to, fold], oback.at[y, fold],
                 s_o.at[i, d], r_o.at[i, d], (other, x * 8 + to))

    def collect(i):
        base = i * FOLD
        fold = pl.ds(base, FOLD)
        for d in range(8):
            at = oback.at[m8(y - d), fold]
            remote(at, at, s_o.at[i, d], r_o.at[i, d], (other, place)).wait_recv()
        half = ROWS // 2
        low_lanes = iota((half, TOK), 1) < 64
        for m in range(4):
            col = m * QD
            for c in range(3):
                r = pl.ds(base + c * ROWS, ROWS)
                oall[pl.ds(i * ROWS, ROWS), pl.ds(col + c * TOK, TOK)] = oback[2 * m, r, :]
                oall[pl.ds(i * ROWS, ROWS), pl.ds(col + 512 + c * TOK, TOK)] = (
                    oback[2 * m + 1, r, :])
            r = pl.ds(base + 3 * ROWS, half)
            even = oback[2 * m, r, :].astype(F32)
            odd = oback[2 * m + 1, r, :].astype(F32)
            oall[pl.ds(i * ROWS, half), pl.ds(col + 384, TOK)] = (
                jnp.where(low_lanes, even, odd).astype(BF))
            oall[pl.ds(i * ROWS + half, half), pl.ds(col + 384, TOK)] = (
                pltpu.roll(jnp.where(low_lanes, odd, even), 64, 1).astype(BF))

    def bounds():
        for d in range(1, 8):
            at = bnd.at[m8(y - d)]
            remote(at, at, s_b.at[d - 1], r_b.at[d - 1], on_line(y + d)).wait_recv()

    def tokens_in(i):
        for k in (0, 4, 5, 6):
            tok_arrived(i, k)

    def partial_out(i, c):
        if c == 0:
            masked_tokens(i)
        partial(i, c)
        p_start(i, c, range(4))

    def pass_weights(n):
        for k in (0, 1):
            w_wait(n, (k,))
            w_start(n, (k + 2,))

    def from_other_core():
        remote(tok, toks, s_sib.at[0], r_sib.at[0], (other, place)).wait_recv()
        remote(dmine, dests, s_sib.at[1], r_sib.at[1], (other, place)).wait_recv()
        remote(smine, scos, s_sib.at[2], r_sib.at[2], (other, place)).wait_recv()

    work = dict(
        F=forward, D=own_weights, B=bounds, T=tokens_in, W=pass_weights, V=w_start,
        X=w_wait, P=partial_out, R=relayed, H=hidden, G=pass_on, O=expert_out,
        S=from_other_core, C=collect)
    for step in ORDER:
        work[step[0]](*step[1:])

    back = onehot(dests[...] == lane.astype(F32)).astype(BF)

    @pl.loop(0, 7)
    def _(c):
        at = pl.ds(pl.multiple_of(c * 512, 512), 512)
        gain = scos[...]
        moved = dot(back, oall[:, at])
        gain = jnp.concatenate([gain] * 4, axis=1)
        out[:, at] = (toks[:, at].astype(F32) + gain * moved).astype(BF)

    for copy in pending:
        copy.wait_send()


def body(tokens, routing, scores, w_gate, w_up, w_down):
    vmem = pl.BlockSpec(memory_space=pltpu.VMEM)
    hbm = pl.BlockSpec(memory_space=pl.ANY)
    dma = pltpu.SemaphoreType.DMA
    result = pl.pallas_call(
        kernel,
        out_shape=jax.ShapeDtypeStruct((TOK, D), BF),
        in_specs=[vmem, vmem, vmem, hbm, hbm, hbm],
        out_specs=vmem,
        scratch_shapes=[
            pltpu.VMEM((4, TOK, QD), BF),
            pltpu.VMEM((8, TOK, QD), BF),
            pltpu.VMEM((8, 8, TOK), F32),
            pltpu.VMEM((8, TOK, 2 * HB), F32),
            pltpu.VMEM((8, TOK, 2 * HB), BF),
            pltpu.VMEM((2, TOK, 2 * HB), BF),
            pltpu.VMEM((2, 2, TOK, 2 * HB), BF),
            pltpu.VMEM((2, 8, TOK, HB), BF),
            pltpu.VMEM((STAGES, 3, 8 * ROWS, QD), BF),
            pltpu.VMEM((3, 8 * ROWS, 2 * HB), BF),
            pltpu.VMEM((4, 2, 2, QD, 256), BF),
            pltpu.VMEM((4, 448, 2 * HB), BF),
            pltpu.VMEM((8, STAGES * FOLD, TOK), BF),
            pltpu.VMEM((8, STAGES * FOLD, TOK), BF),
            pltpu.VMEM((TOK, D), BF),
            pltpu.VMEM((TOK, TOK), F32),
            pltpu.VMEM((TOK, TOK), F32),
            pltpu.VMEM((TOK, TOK), F32),
            pltpu.VMEM((TOK, TOK), F32),
            pltpu.VMEM((TOK, D), BF),
            dma((5,)),
            dma((5, 4)), dma((5, 4)),
            dma((7,)), dma((7,)),
            dma((3,)), dma((3,)),
            dma((STAGES, 7)), dma((STAGES, 7)),
            dma((STAGES, 2, 6)), dma((STAGES, 2, 6)),
            dma((STAGES, 4, 2)), dma((STAGES, 4, 2)),
            dma((STAGES, 8)), dma((STAGES, 8)),
        ],
        compiler_params=pltpu.CompilerParams(
            collective_id=0, has_side_effects=True, vmem_limit_bytes=52 * 2**20),
        cost_estimate=pl.CostEstimate(
            flops=8 * 10**9, bytes_accessed=6 * 10**6, transcendentals=131072),
    )(tokens[0], routing[0], scores[0], w_gate[0, 0], w_up[0, 0], w_down[0, 0].T)
    return result[None]


def solution(mesh):
    return jax.shard_map(
        body,
        mesh=mesh,
        in_specs=(
            P("pipe", "expert", None),
            P("pipe", "expert", None),
            P("pipe", "expert", None),
            P("pipe", "expert", None, None),
            P("pipe", "expert", None, None),
            P("pipe", "expert", None, None),
        ),
        out_specs=P("pipe", "expert", None),
        check_vma=False,
    )
```
